128 devices in a mesh: ia: 16 (over z, x), ja: 8 (over y, core).
Axes of the slice: x: 4, y: 4, z: 4, core: 2. Of those that a mesh axis runs over, the one named last changes fastest.
Arguments:
- amplitudes: bfloat16 [8, 16, 128, 128, 128], P(None, 'ia', 'ja'), may hold values from -6 to 6
- coefficients: bfloat16 [8, 16, 128, 128, 128], P(None, 'ia', 'ja'), may hold values from -0.5 to 0.5
- integrals: bfloat16 [8, 16, 128, 128, 128], P(None, 'ia', 'ja'), may hold values from -6 to 6
- pno_energy: float32 [8, 16, 128, 128], P(None, 'ia', 'ja'), may hold values from 0.5 to 4
- pno_counts: int32 [8, 16, 128], P(None, 'ia', 'ja'), may hold values from 32 to 128
- coupled: int32 [8, 16, 128, 12], P(None, 'ia', 'ja'), may hold values 0 or 1
- occ_fock: float32 [128, 128], replicated, may hold values from -1.5 to 1.5
- occ_energy: float32 [128], replicated, may hold values from -1.5 to -0.3
Outputs:
- amplitudes_next: bfloat16 [8, 16, 128, 128, 128], P(None, 'ia', 'ja')
The draws below stay inside these ranges and needn't reach their ends.
All inputs are finite; a program needn't handle non-finite values. No bound on the sum of `coupled` on one device may be relied on, other than what follows from the above.
Results may differ from the reference program's by a relative error of at most 0.0051.
Values may be sent and summed in bfloat16 or wider, within the bound.
No kernel may reach another device: no remote copies, remote signals or barrier semaphores. Data moves between devices by JAX's collectives and lax.ppermute only.
A program may use at most 128 MiB of HBM per device.

```python
from functools import partial
import jax
import jax.numpy as jnp
from jax import lax

V = 128
WIN = 6
ITERS = 2
BLOCK = 16
BLOCKS = 8
NOCC = 128


def set_ends(drawn, rng, low, top_value):
    dims = drawn.shape
    place = [jax.random.randint(jax.random.fold_in(rng, axis), (), 0, dims[axis]) for axis in range(len(dims))]
    drawn = drawn.at[tuple(place)].set(low)
    longest = dims.index(max(dims))
    place[longest] = (place[longest] + 1) % dims[longest]
    return drawn.at[tuple(place)].set(top_value)


def block_scale(rng, extent, pieces, low, largest):
    level = 1.0
    for dim, blocks in pieces:
        draws = jax.random.uniform(jax.random.fold_in(jax.random.fold_in(rng, 6), dim), (blocks,), jnp.float32, low / len(pieces), largest / len(pieces))
        level = level * jnp.repeat(jnp.exp(draws), extent[dim] // blocks).reshape((-1,) + (1,) * (len(extent) - 1 - dim))
    return level


def gaussian(own_key, shape, deviation, reach, shards=(), held_as=jnp.bfloat16):
    values = jax.random.normal(own_key, shape, jnp.float32) * deviation
    if len(shards) > 0:
        values = block_scale(own_key, shape, shards, -0.22, 0.18) * values
    return jnp.clip(values, min=-reach, max=reach).astype(held_as)


def setup_inputs(seed: int = 0) -> dict:
    seeds = jax.random.split(jax.random.key(seed), 9)
    amplitudes = gaussian(seeds[0], (BLOCKS, BLOCK, NOCC, V, V), 1.0, 6.0, ((1, 16), (2, 8)))
    coefficients = gaussian(seeds[1], (BLOCKS, BLOCK, NOCC, V, V), V ** -0.5, 0.5, ((1, 16), (2, 8)))
    integrals = gaussian(seeds[2], (BLOCKS, BLOCK, NOCC, V, V), 1.0, 6.0, ((1, 16), (2, 8)))
    pno_energy = jnp.clip(0.5 + 3.5 * jax.random.uniform(seeds[3], (BLOCKS, BLOCK, NOCC, V), jnp.float32) ** block_scale(seeds[3], (BLOCKS, BLOCK, NOCC, V), ((1, 16), (2, 8)), -0.2, 0.2), 0.5, 4.0)
    pno_counts = set_ends(jax.random.randint(seeds[4], (BLOCKS, BLOCK, NOCC), V // 4, V + 1), jax.random.fold_in(seeds[4], 1), V // 4, V).astype(jnp.int32)
    coupled = set_ends((jax.random.randint(seeds[5], (BLOCKS, BLOCK, NOCC, 2 * WIN), 0, 4) < 3).astype(jnp.int32), jax.random.fold_in(seeds[5], 1), 0, 1)
    occ_fock = gaussian(seeds[6], (NOCC, NOCC), 0.25, 1.5, (), jnp.float32)
    occ_energy = jnp.clip(jax.random.uniform(seeds[7], (NOCC,), jnp.float32, -1.5, -0.3), -1.5, -0.3)
    return dict(amplitudes=amplitudes, coefficients=coefficients, integrals=integrals, pno_energy=pno_energy, pno_counts=pno_counts, coupled=coupled, occ_fock=occ_fock, occ_energy=occ_energy)


DAMPING = 0.5


def window_shift(slot_index):
    return slot_index - WIN if slot_index < WIN else slot_index - WIN + 1


def rounded(values):
    return lax.optimization_barrier(values.astype(jnp.bfloat16)).astype(jnp.float32)


def fock_band(occ_fock):
    orbitals = occ_fock.shape[0]
    places = jnp.arange(orbitals, dtype=jnp.int32)
    rows_out = []
    for slot_index in range(2 * WIN):
        matches = places[:, None] == places[None, :] + window_shift(slot_index)
        rows_out.append(jnp.sum(jnp.where(matches, occ_fock, jnp.zeros_like(occ_fock)), axis=0))
    return jnp.stack(rows_out, axis=0)


def pair_mask(counts):
    levels = jnp.arange(V, dtype=jnp.int32)
    inside = levels[None, :] < counts[:, None]
    return inside[:, :, None] & inside[:, None, :]


def half_row(packed):
    amp_row, coef_row, integral_row, weights_row = packed
    amps_float = amp_row.astype(jnp.float32)
    coefs_float = coef_row.astype(jnp.float32)
    ints_float = integral_row.astype(jnp.float32)
    orbitals = amp_row.shape[0]
    leading = rounded(jnp.einsum("jab,jbc->jac", coefs_float, amps_float))
    back_form = jnp.einsum("jac,jdc->jad", leading, coefs_float).astype(jnp.bfloat16)
    padded = jnp.pad(back_form, ((WIN, WIN), (0, 0), (0, 0)))
    window_sum = jnp.zeros((orbitals, V, V), jnp.float32)
    for slot_index in range(2 * WIN):
        begin_at = WIN + window_shift(slot_index)
        window_sum = window_sum + weights_row[:, slot_index][:, None, None] * padded[begin_at:begin_at + orbitals].astype(jnp.float32)
    window_bf = rounded(window_sum)
    left_proj = rounded(jnp.einsum("jca,jcd->jad", coefs_float, window_bf))
    projected = jnp.einsum("jad,jde->jae", left_proj, coefs_float)
    left_quad = rounded(jnp.einsum("jab,jbc->jac", amps_float, ints_float))
    quadratic = jnp.einsum("jac,jcd->jad", left_quad, amps_float) / V
    return (0.5 * ints_float + quadratic - projected).astype(jnp.bfloat16)


def update_row(halves, occ_energy, packed):
    row_index, amp_row, energy_row, count_row = packed
    own_half = lax.dynamic_index_in_dim(halves, row_index, 0, keepdims=False)
    partner = lax.dynamic_index_in_dim(halves, row_index, 1, keepdims=False)
    residual = own_half.astype(jnp.float32) + jnp.swapaxes(partner, 1, 2).astype(jnp.float32)
    energy_own = lax.dynamic_index_in_dim(occ_energy, row_index, 0, keepdims=False)
    denominator = energy_row[:, :, None] + energy_row[:, None, :] - energy_own - occ_energy[:, None, None]
    stepped = (1.0 - DAMPING) * amp_row.astype(jnp.float32) - DAMPING * residual / denominator
    return jnp.where(pair_mask(count_row), stepped, jnp.zeros_like(stepped)).astype(jnp.bfloat16)


def mask_row(packed):
    amp_row, count_row = packed
    return jnp.where(pair_mask(count_row), amp_row, jnp.zeros_like(amp_row))


def reference(amplitudes, coefficients, integrals, pno_energy, pno_counts, coupled, occ_fock, occ_energy):
    orbitals = NOCC
    pair_shape = (orbitals, orbitals, V, V)
    amp_pairs = amplitudes.reshape(pair_shape)
    coef_pairs = coefficients.reshape(pair_shape)
    integral_pairs = integrals.reshape(pair_shape)
    energies = pno_energy.reshape(orbitals, orbitals, V)
    counts = pno_counts.reshape(orbitals, orbitals)
    listed = coupled.reshape(orbitals, orbitals, 2 * WIN).astype(jnp.float32)
    weights = listed * jnp.transpose(fock_band(occ_fock))[None, :, :]
    current = lax.map(mask_row, (amp_pairs, counts))
    row_ids = jnp.arange(orbitals, dtype=jnp.int32)
    for sweep in range(ITERS):
        halves = lax.map(half_row, (current, coef_pairs, integral_pairs, weights))
        current = lax.map(partial(update_row, halves, occ_energy), (row_ids, current, energies, counts))
    return current.reshape(amplitudes.shape)
```

```python
from functools import partial

import jax
import jax.numpy as jnp
from jax import lax
from jax.experimental import pallas as pl
from jax.experimental.pallas import tpu as pltpu
from jax.sharding import PartitionSpec as P

WIN = 6
ITERS = 2
DAMPING = 0.5
GROUPS = 2
SKEW = 4
VMEM_BYTES = 16 * 1024 * 1024

BF = jnp.bfloat16
F32 = jnp.float32


def window_shift(slot_index):
    return slot_index - WIN if slot_index < WIN else slot_index - WIN + 1


def nn(a, b):
    return lax.dot_general(a, b, (((1,), (0,)), ((), ())), preferred_element_type=F32)


def nt(a, b):
    return lax.dot_general(a, b, (((1,), (1,)), ((), ())), preferred_element_type=F32)


def tn(a, b):
    return lax.dot_general(a, b, (((0,), (0,)), ((), ())), preferred_element_type=F32)


def inside_mask(count, virtuals):
    rows = lax.broadcasted_iota(jnp.int32, (virtuals, virtuals), 0)
    cols = lax.broadcasted_iota(jnp.int32, (virtuals, virtuals), 1)
    return jnp.maximum(rows, cols) < count


def back_forms(f, amps, coef, x_ref, first_ref, last_ref):
    columns = x_ref.shape[1]
    ready, leading = {}, {}
    for step in range(columns + 2 * SKEW):
        b = step
        if b < columns:
            ready[b] = amps(b)
        b = step - SKEW
        if 0 <= b < columns:
            leading[b] = nn(coef(b), ready.pop(b)).astype(BF)
        b = step - 2 * SKEW
        if 0 <= b:
            back = nt(leading.pop(b), coef(b)).astype(BF)
            x_ref[f, b] = back
            if b < WIN:
                first_ref[f, b] = back
            if b >= columns - WIN:
                last_ref[f, b - (columns - WIN)] = back


def masked_forms(f, offset, counts_ref, raw_ref, c_ref, tm_ref, x_ref, first_ref, last_ref):
    virtuals = x_ref.shape[2]

    def amps(b):
        keep = inside_mask(counts_ref[f + offset, b], virtuals)
        value = jnp.where(keep, raw_ref[f, b].astype(F32), 0.0).astype(BF)
        tm_ref[f, b] = value
        return value

    back_forms(f, amps, lambda b: c_ref[f, b], x_ref, first_ref, last_ref)


def start_kernel(
    counts_ref, t_hbm, c_hbm, tm_ref, c_ref, raw_next, c_next, x_ref, first_ref, last_ref,
    raw_ref, sems, next_sems,
):
    size = x_ref.shape[0]

    def loads(f):
        return (
            pltpu.make_async_copy(t_hbm.at[f, 0], raw_ref.at[f], sems.at[f, 0]),
            pltpu.make_async_copy(c_hbm.at[f, 0], c_ref.at[f], sems.at[f, 1]),
        )

    for f in range(size):
        for load in loads(f):
            load.start()
    rest = pl.ds(size, size)
    later = (
        pltpu.make_async_copy(t_hbm.at[rest, 0], raw_next, next_sems.at[0]),
        pltpu.make_async_copy(c_hbm.at[rest, 0], c_next, next_sems.at[1]),
    )
    for load in later:
        load.start()

    def body(f, carry):
        for load in loads(f):
            load.wait()
        masked_forms(f, 0, counts_ref, raw_ref, c_ref, tm_ref, x_ref, first_ref, last_ref)
        return carry

    lax.fori_loop(0, size, body, 0)
    for load in later:
        load.wait()


def second_kernel(
    counts_ref, raw_ref, c_ref, k_hbm, tm_ref, k_ref, x_ref, first_ref, last_ref, sems
):
    size = x_ref.shape[0]
    load = pltpu.make_async_copy(k_hbm.at[:, 0], k_ref, sems.at[0])
    load.start()

    def body(f, carry):
        masked_forms(f, size, counts_ref, raw_ref, c_ref, tm_ref, x_ref, first_ref, last_ref)
        return carry

    lax.fori_loop(0, size, body, 0)
    load.wait()


def updated(f, b, offset, idx_ref, occ_ref, counts_ref, rows_energy, e_ref, h_ref, p_ref, t_ref):
    columns, virtuals = t_ref.shape[1:3]
    occ_row = occ_ref[(f + offset) * columns + idx_ref[0]]
    occ_col = occ_ref[idx_ref[1] * columns + b]
    cols_energy = e_ref[f + offset, 0, b : b + 1, :]
    denominator = (rows_energy[:, b : b + 1] - occ_row) + (cols_energy - occ_col)
    inverse = pl.reciprocal(denominator)
    residual = h_ref[b, f + offset].astype(F32) + p_ref[b, f + offset].T.astype(F32)
    stepped = (1.0 - DAMPING) * t_ref[f, b].astype(F32) - (DAMPING * residual) * inverse
    keep = inside_mask(counts_ref[f + offset, b], virtuals)
    return jnp.where(keep, stepped, 0.0).astype(BF)


def middle_kernel(
    offset, idx_ref, occ_ref, counts_ref, e_ref, h_ref, p_ref, t_ref, c_ref,
    tm_ref, x_ref, first_ref, last_ref,
):
    def body(f, carry):
        rows_energy = e_ref[f + offset, 0].T

        def amps(b):
            value = updated(
                f, b, offset, idx_ref, occ_ref, counts_ref, rows_energy, e_ref, h_ref, p_ref, t_ref
            )
            tm_ref[f, b] = value
            return value

        back_forms(f, amps, lambda b: c_ref[f, b], x_ref, first_ref, last_ref)
        return carry

    lax.fori_loop(0, x_ref.shape[0], body, 0)


def last_kernel(idx_ref, occ_ref, counts_ref, e_ref, h_ref, p_ref, *rest):
    out_hbm, made_ref, sems = rest[-3:]
    t_refs = rest[:-3]
    size, columns = t_refs[0].shape[:2]

    def store(f):
        return pltpu.make_async_copy(made_ref.at[f], out_hbm.at[f, 0], sems.at[f])

    for g, t_ref in enumerate(t_refs):
        offset = g * size

        def body(f, carry, offset=offset, t_ref=t_ref):
            rows_energy = e_ref[f + offset, 0].T
            for b in range(columns):
                made_ref[f + offset, b] = updated(
                    f, b, offset, idx_ref, occ_ref, counts_ref, rows_energy, e_ref, h_ref, p_ref, t_ref
                )
            store(f + offset).start()
            return carry

        lax.fori_loop(0, size, body, 0)
    for f in range(len(t_refs) * size):
        store(f).wait()


def half_kernel(offset, w_ref, t_ref, c_ref, k_ref, x_ref, before_ref, after_ref, *rest):
    h_ref, xf = rest[-2:]
    size, columns, virtuals = x_ref.shape[:3]
    lag = columns // 2

    def body(f, carry):
        xf[0:WIN] = before_ref[f].astype(F32)
        xf[WIN : WIN + columns] = x_ref[f].astype(F32)
        xf[WIN + columns : 2 * WIN + columns] = after_ref[f].astype(F32)
        window, left_proj, left_quad = {}, {}, {}
        for step in range(columns + 2 * lag):
            b = step
            if b < columns:
                total = w_ref[f + offset, b * 2 * WIN] * xf[b + WIN + window_shift(0)]
                for s in range(1, 2 * WIN):
                    total = total + w_ref[f + offset, b * 2 * WIN + s] * xf[b + WIN + window_shift(s)]
                window[b] = total.astype(BF)
            b = step - lag
            if 0 <= b < columns:
                left_proj[b] = tn(c_ref[f, b], window.pop(b)).astype(BF)
                left_quad[b] = (nn(t_ref[f, b], k_ref[f + offset, b]) * (1.0 / virtuals)).astype(BF)
            b = step - 2 * lag
            if 0 <= b:
                joined = nn(
                    jnp.concatenate([left_quad.pop(b), -left_proj.pop(b)], axis=1),
                    jnp.concatenate([t_ref[f, b], c_ref[f, b]], axis=0),
                )
                h_ref[b, f + offset] = (0.5 * k_ref[f + offset, b].astype(F32) + joined).astype(BF)
        return carry

    lax.fori_loop(0, size, body, 0)


SMEM = pl.BlockSpec(memory_space=pltpu.SMEM)
VMEM = pl.BlockSpec(memory_space=pltpu.VMEM)
HBM = pl.BlockSpec(memory_space=pltpu.HBM)


def params():
    return pltpu.CompilerParams(vmem_limit_bytes=VMEM_BYTES)


def near_core(value):
    return pltpu.with_memory_space_constraint(value, pltpu.VMEM)


def far(value):
    return pltpu.with_memory_space_constraint(value, pltpu.HBM)


def cost(flops, moved):
    return pl.CostEstimate(flops=flops, bytes_accessed=moved, transcendentals=0)


def on_device(
    amplitudes, coefficients, integrals, pno_energy, pno_counts, coupled, occ_fock, occ_energy
):
    fragments, _, columns, virtuals, _ = amplitudes.shape
    size = fragments // GROUPS
    pairs = size * columns
    matmul = 2 * virtuals**3 * pairs
    block = 2 * virtuals**2 * pairs
    col_dev = lax.axis_index("ja")
    idx = jnp.stack([lax.axis_index("ia"), col_dev]).astype(jnp.int32)
    counts = pno_counts.reshape(fragments, columns)
    near = lax.dynamic_slice(
        jnp.pad(occ_fock, ((WIN, WIN), (0, 0))),
        (col_dev * columns, col_dev * columns),
        (columns + 2 * WIN, columns),
    )
    reach = jnp.arange(columns + 2 * WIN)[None, None, :]
    place = jnp.arange(columns)[:, None, None]
    shifts = jnp.array([window_shift(s) + WIN for s in range(2 * WIN)])[None, :, None]
    band = jnp.sum(jnp.where(reach == place + shifts, jnp.transpose(near)[:, None, :], 0.0), axis=2)
    weights = (coupled.astype(F32) * band[None, None]).reshape(fragments, columns * 2 * WIN)
    weights, idx, counts, amplitudes = lax.optimization_barrier((weights, idx, counts, amplitudes))
    energies = near_core(pno_energy)

    peers = lax.axis_size("ja")
    up = [(i, i + 1) for i in range(peers - 1)]
    down = [(j, i) for i, j in up]

    def near_shape(*lead):
        return pltpu.VMEM((*lead, virtuals, virtuals), BF)

    group = near_shape(size, columns)
    back = [group, near_shape(size, WIN), near_shape(size, WIN)]

    def first_steps():
        tm, c, raw_next, c_next, *made = pl.pallas_call(
            start_kernel,
            in_specs=[SMEM, HBM, HBM],
            out_shape=[group] * 4 + back,
            out_specs=[VMEM] * 7,
            scratch_shapes=[
                pltpu.VMEM((size, columns, virtuals, virtuals), BF),
                pltpu.SemaphoreType.DMA((size, 2)),
                pltpu.SemaphoreType.DMA((2,)),
            ],
            compiler_params=params(),
            cost_estimate=cost(2 * matmul, 4 * block),
            name="start",
        )(counts, far(amplitudes), far(coefficients))
        borders = [exchange(made)]
        tm_next, k, *made_next = pl.pallas_call(
            second_kernel,
            in_specs=[SMEM, VMEM, VMEM, HBM],
            out_shape=[group, near_shape(fragments, columns)] + back,
            out_specs=[VMEM] * 5,
            scratch_shapes=[pltpu.SemaphoreType.DMA((1,))],
            compiler_params=params(),
            cost_estimate=cost(2 * matmul, 2 * block),
            name="second",
        )(counts, near_core(raw_next), near_core(c_next), far(integrals))
        borders.append(exchange(made_next))
        return [tm, tm_next], [c, c_next], k, [made[0], made_next[0]], borders

    def exchange(made):
        return lax.ppermute(made[2], "ja", up), lax.ppermute(made[1], "ja", down)

    def next_step(g, halves, partner, current, coefs):
        return pl.pallas_call(
            partial(middle_kernel, g * size),
            in_specs=[SMEM] * 3 + [VMEM] * 5,
            out_shape=[group] + back,
            out_specs=[VMEM] * 4,
            compiler_params=params(),
            cost_estimate=cost(2 * matmul, block),
            name="middle",
        )(
            idx, occ_energy, counts, energies, near_core(halves), near_core(partner),
            near_core(current[g]), near_core(coefs[g]),
        )

    def half_step(g, current, coefs, ints, back_form, before, after, out):
        operands = [current[g], coefs[g], ints, back_form, before, after]
        aliases = {}
        if out is not None:
            aliases = {len(operands) + 1: 0}
            operands.append(out)
        return pl.pallas_call(
            partial(half_kernel, g * size),
            in_specs=[SMEM] + [VMEM] * len(operands),
            out_shape=near_shape(columns, fragments),
            out_specs=VMEM,
            scratch_shapes=[pltpu.VMEM((columns + 2 * WIN, virtuals, virtuals), F32)],
            input_output_aliases=aliases,
            compiler_params=params(),
            cost_estimate=cost(4 * matmul, 2 * block),
            name="half",
        )(weights, *map(near_core, operands))

    def last_step(halves, partner, current):
        return pl.pallas_call(
            last_kernel,
            in_specs=[SMEM] * 3 + [VMEM] * (3 + GROUPS),
            out_shape=pltpu.HBM(amplitudes.shape, BF),
            out_specs=HBM,
            scratch_shapes=[
                pltpu.VMEM((fragments, columns, virtuals, virtuals), BF),
                pltpu.SemaphoreType.DMA((fragments,)),
            ],
            compiler_params=params(),
            cost_estimate=cost(0, 2 * GROUPS * block),
            name="last",
        )(
            idx, occ_energy, counts, energies, near_core(halves), near_core(partner),
            *map(near_core, current),
        )

    halves = partner = None
    for sweep in range(ITERS):
        if sweep == 0:
            current, coefs, ints, back_form, borders = first_steps()
        else:
            new, back_form, borders = [], [], []
            for g in range(GROUPS):
                tm, *made = next_step(g, halves, partner, current, coefs)
                borders.append(exchange(made))
                new.append(tm)
                back_form.append(made[0])
            current = new
        halves = None
        for g in range(GROUPS):
            halves = half_step(g, current, coefs, ints, back_form[g], *borders[g], halves)
        sent = halves.reshape(columns * fragments, 1, virtuals, virtuals)
        arrived = lax.all_to_all(sent, ("ia", "ja"), split_axis=0, concat_axis=0, tiled=True)
        partner = arrived.reshape(columns, fragments, virtuals, virtuals)
    return last_step(halves, partner, current)


def solution(mesh):
    placed = (
        P(None, "ia", "ja", None, None),
        P(None, "ia", "ja", None, None),
        P(None, "ia", "ja", None, None),
        P(None, "ia", "ja", None),
        P(None, "ia", "ja"),
        P(None, "ia", "ja", None),
        P(),
        P(),
    )
    return jax.shard_map(
        on_device,
        mesh=mesh,
        in_specs=placed,
        out_specs=P(None, "ia", "ja", None, None),
        check_vma=False,
    )
```

```python
from functools import partial

import jax
import jax.numpy as jnp
from jax import lax
from jax.experimental import pallas as pl
from jax.experimental.pallas import tpu as pltpu
from jax.sharding import PartitionSpec as P

WIN = 6
ITERS = 2
DAMPING = 0.5
GROUPS = 2
SKEW = 4
VMEM_BYTES = 16 * 1024 * 1024

BF = jnp.bfloat16
F32 = jnp.float32


def window_shift(slot_index):
    return slot_index - WIN if slot_index < WIN else slot_index - WIN + 1


def nn(a, b):
    return lax.dot_general(a, b, (((1,), (0,)), ((), ())), preferred_element_type=F32)


def nt(a, b):
    return lax.dot_general(a, b, (((1,), (1,)), ((), ())), preferred_element_type=F32)


def tn(a, b):
    return lax.dot_general(a, b, (((0,), (0,)), ((), ())), preferred_element_type=F32)


def inside_mask(count, virtuals):
    rows = lax.broadcasted_iota(jnp.int32, (virtuals, virtuals), 0)
    cols = lax.broadcasted_iota(jnp.int32, (virtuals, virtuals), 1)
    return jnp.maximum(rows, cols) < count


def back_forms(f, parity, amps, coef, x_ref, near_ref, far_ref):
    columns = x_ref.shape[1]
    ready, leading = {}, {}
    for step in range(columns + 2 * SKEW):
        b = step
        if b < columns:
            ready[b] = amps(b)
        b = step - SKEW
        if 0 <= b < columns:
            leading[b] = nn(coef(b), ready.pop(b)).astype(BF)
        b = step - 2 * SKEW
        if 0 <= b:
            x_ref[f, b] = nt(leading.pop(b), coef(b)).astype(BF)
    edge = columns - WIN
    near_ref[f] = x_ref[f, pl.ds((1 - parity) * edge, WIN)]
    far_ref[f] = x_ref[f, pl.ds(parity * edge, WIN)]


def masked_forms(f, offset, parity, counts_ref, raw_ref, c_ref, tm_ref, x_ref, near_ref, far_ref):
    virtuals = x_ref.shape[2]

    def amps(b):
        keep = inside_mask(counts_ref[f + offset, 0, b], virtuals)
        value = jnp.where(keep, raw_ref[f, b].astype(F32), 0.0).astype(BF)
        tm_ref[f, b] = value
        return value

    back_forms(f, parity, amps, lambda b: c_ref[f, b], x_ref, near_ref, far_ref)


def start_kernel(
    counts_hbm, t_hbm, c_hbm, tm_ref, c_ref, raw_next, c_next, x_ref, near_ref, far_ref,
    raw_ref, counts_ref, sems, next_sems,
):
    size = x_ref.shape[0]
    parity = lax.rem(lax.axis_index("ja"), 2)

    def loads(f):
        return (
            pltpu.make_async_copy(t_hbm.at[f, 0], raw_ref.at[f], sems.at[f, 0]),
            pltpu.make_async_copy(c_hbm.at[f, 0], c_ref.at[f], sems.at[f, 1]),
        )

    for f in range(size):
        for load in loads(f):
            load.start()
    number = pltpu.make_async_copy(counts_hbm, counts_ref, next_sems.at[2])
    number.start()
    rest = pl.ds(size, size)
    later = (
        pltpu.make_async_copy(t_hbm.at[rest, 0], raw_next, next_sems.at[0]),
        pltpu.make_async_copy(c_hbm.at[rest, 0], c_next, next_sems.at[1]),
    )
    for load in later:
        load.start()
    number.wait()

    def body(f, carry):
        for load in loads(f):
            load.wait()
        masked_forms(f, 0, parity, counts_ref, raw_ref, c_ref, tm_ref, x_ref, near_ref, far_ref)
        return carry

    lax.fori_loop(0, size, body, 0)
    for load in later:
        load.wait()


def second_kernel(
    counts_ref, raw_ref, c_ref, k_hbm, tm_ref, k_ref, x_ref, near_ref, far_ref, sems
):
    size = x_ref.shape[0]
    parity = lax.rem(lax.axis_index("ja"), 2)
    load = pltpu.make_async_copy(k_hbm.at[:, 0], k_ref, sems.at[0])
    load.start()

    def body(f, carry):
        masked_forms(f, size, parity, counts_ref, raw_ref, c_ref, tm_ref, x_ref, near_ref, far_ref)
        return carry

    lax.fori_loop(0, size, body, 0)
    load.wait()


def updated(f, b, offset, occ_ref, counts_ref, rows_energy, e_ref, h_ref, p_ref, t_ref):
    columns, virtuals = t_ref.shape[1:3]
    occ_row = occ_ref[(f + offset) * columns + lax.axis_index("ia")]
    occ_col = occ_ref[lax.axis_index("ja") * columns + b]
    cols_energy = e_ref[f + offset, 0, b : b + 1, :]
    denominator = (rows_energy[:, b : b + 1] - occ_row) + (cols_energy - occ_col)
    inverse = pl.reciprocal(denominator)
    residual = h_ref[b, f + offset].astype(F32) + p_ref[b, f + offset].T.astype(F32)
    stepped = (1.0 - DAMPING) * t_ref[f, b].astype(F32) - (DAMPING * residual) * inverse
    keep = inside_mask(counts_ref[f + offset, 0, b], virtuals)
    return jnp.where(keep, stepped, 0.0).astype(BF)


def middle_kernel(
    offset, occ_ref, counts_ref, e_ref, h_ref, p_ref, t_ref, c_ref,
    tm_ref, x_ref, near_ref, far_ref,
):
    parity = lax.rem(lax.axis_index("ja"), 2)

    def body(f, carry):
        rows_energy = e_ref[f + offset, 0].T

        def amps(b):
            value = updated(
                f, b, offset, occ_ref, counts_ref, rows_energy, e_ref, h_ref, p_ref, t_ref
            )
            tm_ref[f, b] = value
            return value

        back_forms(f, parity, amps, lambda b: c_ref[f, b], x_ref, near_ref, far_ref)
        return carry

    lax.fori_loop(0, x_ref.shape[0], body, 0)


def last_kernel(occ_ref, counts_ref, e_ref, h_ref, p_ref, *rest):
    out_hbm, made_ref, sems = rest[-3:]
    t_refs = rest[:-3]
    size, columns = t_refs[0].shape[:2]

    def store(f):
        return pltpu.make_async_copy(made_ref.at[f], out_hbm.at[f, 0], sems.at[f])

    for g, t_ref in enumerate(t_refs):
        offset = g * size

        def body(f, carry, offset=offset, t_ref=t_ref):
            rows_energy = e_ref[f + offset, 0].T
            for b in range(columns):
                made_ref[f + offset, b] = updated(
                    f, b, offset, occ_ref, counts_ref, rows_energy, e_ref, h_ref, p_ref, t_ref
                )
            store(f + offset).start()
            return carry

        lax.fori_loop(0, size, body, 0)
    for f in range(len(t_refs) * size):
        store(f).wait()


def weights_kernel(coupled_ref, fock_ref, w_ref):
    orbitals = fock_ref.shape[0]
    slots, columns = 2 * WIN, coupled_ref.shape[2]
    rows = lax.broadcasted_iota(jnp.int32, (orbitals, orbitals), 0)
    cols = lax.broadcasted_iota(jnp.int32, (orbitals, orbitals), 1)
    turn = lax.rem(orbitals - lax.axis_index("ja") * columns, orbitals)
    for s in range(slots):
        band = jnp.where(rows == cols + window_shift(s), fock_ref[...], 0.0)
        band = pltpu.roll(jnp.sum(band, axis=0, keepdims=True), turn, 1)[:, :columns]
        for f in range(coupled_ref.shape[0] // slots):
            w_ref[f * slots + s] = -(coupled_ref[f * slots + s].astype(F32) * band)


def half_kernel(offset, w_ref, t_ref, c_ref, k_ref, x_ref, near_ref, far_ref, *rest):
    h_ref, xf = rest[-2:]
    size, columns, virtuals = x_ref.shape[:3]
    lag = columns // 2
    parity = lax.rem(lax.axis_index("ja"), 2)

    def body(f, carry):
        xf[pl.ds((1 - parity) * (WIN + columns), WIN)] = near_ref[f].astype(F32)
        xf[pl.ds(parity * (WIN + columns), WIN)] = far_ref[f].astype(F32)
        xf[WIN : WIN + columns] = x_ref[f].astype(F32)
        window, left_proj, left_quad = {}, {}, {}
        for step in range(columns + 2 * lag):
            b = step
            if b < columns:
                total = w_ref[(f + offset) * 2 * WIN, 0, b] * xf[b + WIN + window_shift(0)]
                for s in range(1, 2 * WIN):
                    total = total + w_ref[(f + offset) * 2 * WIN + s, 0, b] * xf[b + WIN + window_shift(s)]
                window[b] = total.astype(BF)
            b = step - lag
            if 0 <= b < columns:
                left_proj[b] = tn(c_ref[f, b], window.pop(b)).astype(BF)
                left_quad[b] = (nn(t_ref[f, b], k_ref[f + offset, b]) * (1.0 / virtuals)).astype(BF)
            b = step - 2 * lag
            if 0 <= b:
                joined = nn(
                    jnp.concatenate([left_quad.pop(b), left_proj.pop(b)], axis=1),
                    jnp.concatenate([t_ref[f, b], c_ref[f, b]], axis=0),
                )
                h_ref[b, f + offset] = (0.5 * k_ref[f + offset, b].astype(F32) + joined).astype(BF)
        return carry

    lax.fori_loop(0, size, body, 0)


SMEM = pl.BlockSpec(memory_space=pltpu.SMEM)
VMEM = pl.BlockSpec(memory_space=pltpu.VMEM)
HBM = pl.BlockSpec(memory_space=pltpu.HBM)


def params():
    return pltpu.CompilerParams(vmem_limit_bytes=VMEM_BYTES)


def near_core(value):
    return pltpu.with_memory_space_constraint(value, pltpu.VMEM)


def far(value):
    return pltpu.with_memory_space_constraint(value, pltpu.HBM)


def cost(flops, moved):
    return pl.CostEstimate(flops=flops, bytes_accessed=moved, transcendentals=0)


def on_device(
    amplitudes, coefficients, integrals, pno_energy, pno_counts, coupled, occ_fock, occ_energy
):
    fragments, _, columns, virtuals, _ = amplitudes.shape
    size = fragments // GROUPS
    pairs = size * columns
    matmul = 2 * virtuals**3 * pairs
    block = 2 * virtuals**2 * pairs
    listed = jnp.transpose(coupled, (0, 3, 1, 2)).reshape(fragments * 2 * WIN, 1, columns)
    counts = pno_counts
    energies = near_core(pno_energy)

    peers = lax.axis_size("ja")
    near_pairs = [(i, i ^ 1) for i in range(peers)]
    far_pairs = [(i, i + 1 if i % 2 else i - 1) for i in range(1, peers - 1)]

    def near_shape(*lead):
        return pltpu.VMEM((*lead, virtuals, virtuals), BF)

    group = near_shape(size, columns)
    back = [group, near_shape(size, WIN), near_shape(size, WIN)]

    def first_steps():
        tm, c, raw_next, c_next, *made = pl.pallas_call(
            start_kernel,
            in_specs=[HBM, HBM, HBM],
            out_shape=[group] * 4 + back,
            out_specs=[VMEM] * 7,
            scratch_shapes=[
                pltpu.VMEM((size, columns, virtuals, virtuals), BF),
                pltpu.SMEM(counts.shape, jnp.int32),
                pltpu.SemaphoreType.DMA((size, 2)),
                pltpu.SemaphoreType.DMA((3,)),
            ],
            compiler_params=params(),
            cost_estimate=cost(2 * matmul, 4 * block),
            name="start",
        )(far(counts), far(amplitudes), far(coefficients))
        borders = [exchange(made)]
        tm_next, k, *made_next = pl.pallas_call(
            second_kernel,
            in_specs=[SMEM, VMEM, VMEM, HBM],
            out_shape=[group, near_shape(fragments, columns)] + back,
            out_specs=[VMEM] * 5,
            scratch_shapes=[pltpu.SemaphoreType.DMA((1,))],
            compiler_params=params(),
            cost_estimate=cost(2 * matmul, 2 * block),
            name="second",
        )(counts, near_core(raw_next), near_core(c_next), far(integrals))
        borders.append(exchange(made_next))
        weights = pl.pallas_call(
            weights_kernel,
            in_specs=[VMEM, VMEM],
            out_shape=jax.ShapeDtypeStruct(listed.shape, F32),
            out_specs=VMEM,
            compiler_params=params(),
            cost_estimate=cost(0, block // 8),
            name="weights",
        )(*lax.optimization_barrier((listed, occ_fock, tm_next))[:2])
        return [tm, tm_next], [c, c_next], k, [made[0], made_next[0]], borders, weights

    def exchange(made):
        return lax.ppermute(made[1], "ja", near_pairs), lax.ppermute(made[2], "ja", far_pairs)

    def next_step(g, halves, partner, current, coefs):
        return pl.pallas_call(
            partial(middle_kernel, g * size),
            in_specs=[SMEM] * 2 + [VMEM] * 5,
            out_shape=[group] + back,
            out_specs=[VMEM] * 4,
            compiler_params=params(),
            cost_estimate=cost(2 * matmul, block),
            name="middle",
        )(
            occ_energy, counts, energies, near_core(halves), near_core(partner),
            near_core(current[g]), near_core(coefs[g]),
        )

    def half_step(g, weights, current, coefs, ints, back_form, from_near, from_far, out):
        operands = [current[g], coefs[g], ints, back_form, from_near, from_far]
        aliases = {}
        if out is not None:
            aliases = {len(operands) + 1: 0}
            operands.append(out)
        return pl.pallas_call(
            partial(half_kernel, g * size),
            in_specs=[SMEM] + [VMEM] * len(operands),
            out_shape=near_shape(columns, fragments),
            out_specs=VMEM,
            scratch_shapes=[pltpu.VMEM((columns + 2 * WIN, virtuals, virtuals), F32)],
            input_output_aliases=aliases,
            compiler_params=params(),
            cost_estimate=cost(4 * matmul, 2 * block),
            name="half",
        )(weights, *map(near_core, operands))

    def last_step(halves, partner, current):
        return pl.pallas_call(
            last_kernel,
            in_specs=[SMEM] * 2 + [VMEM] * (3 + GROUPS),
            out_shape=pltpu.HBM(amplitudes.shape, BF),
            out_specs=HBM,
            scratch_shapes=[
                pltpu.VMEM((fragments, columns, virtuals, virtuals), BF),
                pltpu.SemaphoreType.DMA((fragments,)),
            ],
            compiler_params=params(),
            cost_estimate=cost(0, 2 * GROUPS * block),
            name="last",
        )(
            occ_energy, counts, energies, near_core(halves), near_core(partner),
            *map(near_core, current),
        )

    halves = partner = None
    for sweep in range(ITERS):
        if sweep == 0:
            current, coefs, ints, back_form, borders, weights = first_steps()
        else:
            new, back_form, borders = [], [], []
            for g in range(GROUPS):
                tm, *made = next_step(g, halves, partner, current, coefs)
                borders.append(exchange(made))
                new.append(tm)
                back_form.append(made[0])
            current = new
        halves = None
        for g in range(GROUPS):
            halves = half_step(g, weights, current, coefs, ints, back_form[g], *borders[g], halves)
        sent = halves.reshape(columns * fragments, 1, virtuals, virtuals)
        arrived = lax.all_to_all(sent, ("ia", "ja"), split_axis=0, concat_axis=0, tiled=True)
        partner = arrived.reshape(columns, fragments, virtuals, virtuals)
    return last_step(halves, partner, current)


def solution(mesh):
    placed = (
        P(None, "ia", "ja", None, None),
        P(None, "ia", "ja", None, None),
        P(None, "ia", "ja", None, None),
        P(None, "ia", "ja", None),
        P(None, "ia", "ja"),
        P(None, "ia", "ja", None),
        P(),
        P(),
    )
    return jax.shard_map(
        on_device,
        mesh=mesh,
        in_specs=placed,
        out_specs=P(None, "ia", "ja", None, None),
        check_vma=False,
    )
```

```python
from functools import partial

import jax
import jax.numpy as jnp
from jax import lax
from jax.experimental import pallas as pl
from jax.experimental.pallas import tpu as pltpu
from jax.sharding import PartitionSpec as P

WIN = 6
ITERS = 2
DAMPING = 0.5
GROUPS = ((4, 4), (4, 2, 2))
SKEW = 4
VMEM_BYTES = 16 * 1024 * 1024

BF = jnp.bfloat16
F32 = jnp.float32


def window_shift(slot_index):
    return slot_index - WIN if slot_index < WIN else slot_index - WIN + 1


def nn(a, b):
    return lax.dot_general(a, b, (((1,), (0,)), ((), ())), preferred_element_type=F32)


def nt(a, b):
    return lax.dot_general(a, b, (((1,), (1,)), ((), ())), preferred_element_type=F32)


def tn(a, b):
    return lax.dot_general(a, b, (((0,), (0,)), ((), ())), preferred_element_type=F32)


def inside_mask(count, virtuals):
    rows = lax.broadcasted_iota(jnp.int32, (virtuals, virtuals), 0)
    cols = lax.broadcasted_iota(jnp.int32, (virtuals, virtuals), 1)
    return jnp.maximum(rows, cols) < count


def back_forms(f, parity, amps, coef, x_ref, near_ref, far_ref):
    columns = x_ref.shape[1]
    ready, leading = {}, {}
    for step in range(columns + 2 * SKEW):
        b = step
        if b < columns:
            ready[b] = amps(b)
        b = step - SKEW
        if 0 <= b < columns:
            leading[b] = nn(coef(b), ready.pop(b)).astype(BF)
        b = step - 2 * SKEW
        if 0 <= b:
            x_ref[f, b] = nt(leading.pop(b), coef(b)).astype(BF)
    edge = columns - WIN
    near_ref[f] = x_ref[f, pl.ds((1 - parity) * edge, WIN)]
    far_ref[f] = x_ref[f, pl.ds(parity * edge, WIN)]


def masked_forms(f, offset, parity, counts_ref, raw_ref, c_ref, tm_ref, x_ref, near_ref, far_ref):
    virtuals = x_ref.shape[2]

    def amps(b):
        keep = inside_mask(counts_ref[f + offset, 0, b], virtuals)
        value = jnp.where(keep, raw_ref[f, b].astype(F32), 0.0).astype(BF)
        tm_ref[f, b] = value
        return value

    back_forms(f, parity, amps, lambda b: c_ref[f, b], x_ref, near_ref, far_ref)


def start_kernel(
    counts_hbm, t_hbm, c_hbm, tm_ref, c_ref, raw_next, c_next, x_ref, near_ref, far_ref,
    raw_ref, counts_ref, sems, next_sems,
):
    size = x_ref.shape[0]
    parity = lax.rem(lax.axis_index("ja"), 2)

    def loads(f):
        return (
            pltpu.make_async_copy(t_hbm.at[f, 0], raw_ref.at[f], sems.at[f, 0]),
            pltpu.make_async_copy(c_hbm.at[f, 0], c_ref.at[f], sems.at[f, 1]),
        )

    for f in range(size):
        for load in loads(f):
            load.start()
    number = pltpu.make_async_copy(counts_hbm, counts_ref, next_sems.at[2])
    number.start()
    rest = pl.ds(size, size)
    later = (
        pltpu.make_async_copy(t_hbm.at[rest, 0], raw_next, next_sems.at[0]),
        pltpu.make_async_copy(c_hbm.at[rest, 0], c_next, next_sems.at[1]),
    )
    for load in later:
        load.start()
    number.wait()

    def body(f, carry):
        for load in loads(f):
            load.wait()
        masked_forms(f, 0, parity, counts_ref, raw_ref, c_ref, tm_ref, x_ref, near_ref, far_ref)
        return carry

    lax.fori_loop(0, size, body, 0)
    for load in later:
        load.wait()


def second_kernel(
    counts_ref, raw_ref, c_ref, k_hbm, tm_ref, k_ref, x_ref, near_ref, far_ref, sems
):
    size = x_ref.shape[0]
    parity = lax.rem(lax.axis_index("ja"), 2)
    load = pltpu.make_async_copy(k_hbm.at[:, 0], k_ref, sems.at[0])
    load.start()

    def body(f, carry):
        masked_forms(f, size, parity, counts_ref, raw_ref, c_ref, tm_ref, x_ref, near_ref, far_ref)
        return carry

    lax.fori_loop(0, size, body, 0)
    load.wait()


def gain_kernel(occ_ref, counts_ref, e_ref, coupled_ref, fock_ref, gain_ref, w_ref):
    orbitals = fock_ref.shape[0]
    fragments, columns, virtuals = gain_ref.shape[:3]
    slots = 2 * WIN
    rows = lax.broadcasted_iota(jnp.int32, (orbitals, orbitals), 0)
    cols = lax.broadcasted_iota(jnp.int32, (orbitals, orbitals), 1)
    turn = lax.rem(orbitals - lax.axis_index("ja") * columns, orbitals)
    for s in range(slots):
        band = jnp.where(rows == cols + window_shift(s), fock_ref[...], 0.0)
        band = pltpu.roll(jnp.sum(band, axis=0, keepdims=True), turn, 1)[:, :columns]
        parts = [coupled_ref[f * slots + s].astype(F32) * band for f in range(fragments)]
        w_ref[s : s + 1, :] = -jnp.concatenate(parts, axis=1)

    def body(f, carry):
        rows_energy = e_ref[f, 0].T
        occ_row = occ_ref[f * columns + lax.axis_index("ia")]
        for b in range(columns):
            occ_col = occ_ref[lax.axis_index("ja") * columns + b]
            cols_energy = e_ref[f, 0, b : b + 1, :] - occ_col
            denominator = (rows_energy[:, b : b + 1] - occ_row) + cols_energy
            keep = inside_mask(counts_ref[f, 0, b], virtuals)
            gain_ref[f, b] = jnp.where(keep, DAMPING * pl.reciprocal(denominator), 0.0)
        return carry

    lax.fori_loop(0, fragments, body, 0)


def updated(f, b, amps, gain_ref, h_ref, p_ref):
    residual = h_ref[b, f].astype(F32) + p_ref[b, f].T.astype(F32)
    return ((1.0 - DAMPING) * amps.astype(F32) - gain_ref[f, b] * residual).astype(BF)


def middle_kernel(
    offset, inner, gain_ref, h_ref, p_ref, t_ref, c_ref,
    tm_ref, x_ref, near_ref, far_ref,
):
    parity = lax.rem(lax.axis_index("ja"), 2)

    def body(f, carry):
        def amps(b):
            value = updated(f + offset, b, t_ref[f + inner, b], gain_ref, h_ref, p_ref)
            tm_ref[f, b] = value
            return value

        back_forms(f, parity, amps, lambda b: c_ref[f + inner, b], x_ref, near_ref, far_ref)
        return carry

    lax.fori_loop(0, x_ref.shape[0], body, 0)


def last_kernel(gain_ref, h_ref, p_ref, *rest):
    out_hbm, made_ref, sems = rest[-3:]
    columns = made_ref.shape[1]

    def store(f):
        return pltpu.make_async_copy(made_ref.at[f], out_hbm.at[f, 0], sems.at[f])

    offset = 0
    for t_ref in rest[:-3]:

        def body(f, carry, offset=offset, t_ref=t_ref):
            for b in range(columns):
                made_ref[f + offset, b] = updated(
                    f + offset, b, t_ref[f, b], gain_ref, h_ref, p_ref
                )
            store(f + offset).start()
            return carry

        lax.fori_loop(0, t_ref.shape[0], body, 0)
        offset += t_ref.shape[0]
    for f in range(offset):
        store(f).wait()


def left_quads(amps, ints):
    return (nn(amps, ints) * (1.0 / amps.shape[0])).astype(BF)


def half_kernel(offset, inner, w_ref, t_ref, c_ref, k_ref, x_ref, near_ref, far_ref, *rest):
    h_ref, xf = rest[-2:]
    size, columns, virtuals = x_ref.shape[:3]
    lag = columns // 2
    parity = lax.rem(lax.axis_index("ja"), 2)

    def body(f, carry):
        xf[pl.ds((1 - parity) * (WIN + columns), WIN)] = near_ref[f].astype(F32)
        xf[pl.ds(parity * (WIN + columns), WIN)] = far_ref[f].astype(F32)
        xf[WIN : WIN + columns] = x_ref[f].astype(F32)
        window, left_proj, left_quad = {}, {}, {}
        for step in range(columns + 2 * lag):
            b = step
            if b < columns:
                total = w_ref[0, (f + offset) * columns + b] * xf[b + WIN + window_shift(0)]
                for s in range(1, 2 * WIN):
                    total = total + w_ref[s, (f + offset) * columns + b] * xf[b + WIN + window_shift(s)]
                window[b] = total.astype(BF)
            b = step - lag
            if 0 <= b < columns:
                left_proj[b] = tn(c_ref[f + inner, b], window.pop(b)).astype(BF)
                left_quad[b] = left_quads(t_ref[f, b], k_ref[f + offset, b])
            b = step - 2 * lag
            if 0 <= b:
                joined = nn(
                    jnp.concatenate([left_quad.pop(b), left_proj.pop(b)], axis=1),
                    jnp.concatenate([t_ref[f, b], c_ref[f + inner, b]], axis=0),
                )
                h_ref[b, f + offset] = (0.5 * k_ref[f + offset, b].astype(F32) + joined).astype(BF)
        return carry

    lax.fori_loop(0, size, body, 0)


SMEM = pl.BlockSpec(memory_space=pltpu.SMEM)
VMEM = pl.BlockSpec(memory_space=pltpu.VMEM)
HBM = pl.BlockSpec(memory_space=pltpu.HBM)


def params():
    return pltpu.CompilerParams(vmem_limit_bytes=VMEM_BYTES)


def near_core(value):
    return pltpu.with_memory_space_constraint(value, pltpu.VMEM)


def far(value):
    return pltpu.with_memory_space_constraint(value, pltpu.HBM)


def cost(flops, moved):
    return pl.CostEstimate(flops=flops, bytes_accessed=moved, transcendentals=0)


def on_device(
    amplitudes, coefficients, integrals, pno_energy, pno_counts, coupled, occ_fock, occ_energy
):
    fragments, _, columns, virtuals, _ = amplitudes.shape
    size = fragments // 2
    pairs = size * columns
    matmul = 2 * virtuals**3 * pairs
    block = 2 * virtuals**2 * pairs
    listed = jnp.transpose(coupled, (0, 3, 1, 2)).reshape(fragments * 2 * WIN, 1, columns)
    counts = pno_counts

    peers = lax.axis_size("ja")
    near_pairs = [(i, i ^ 1) for i in range(peers)]
    far_pairs = [(i, i + 1 if i % 2 else i - 1) for i in range(1, peers - 1)]

    def near_shape(*lead):
        return pltpu.VMEM((*lead, virtuals, virtuals), BF)

    def back_shapes(n):
        return [near_shape(n, m) for m in (columns, WIN, WIN)]

    group, back = near_shape(size, columns), back_shapes(size)

    def first_steps():
        tm, c, raw_next, c_next, *made = pl.pallas_call(
            start_kernel,
            in_specs=[HBM, HBM, HBM],
            out_shape=[group] * 4 + back,
            out_specs=[VMEM] * 7,
            scratch_shapes=[
                pltpu.VMEM((size, columns, virtuals, virtuals), BF),
                pltpu.SMEM(counts.shape, jnp.int32),
                pltpu.SemaphoreType.DMA((size, 2)),
                pltpu.SemaphoreType.DMA((3,)),
            ],
            compiler_params=params(),
            cost_estimate=cost(2 * matmul, 4 * block),
            name="start",
        )(far(counts), far(amplitudes), far(coefficients))
        borders = [exchange(made)]
        tm_next, k, *made_next = pl.pallas_call(
            second_kernel,
            in_specs=[SMEM, VMEM, VMEM, HBM],
            out_shape=[group, near_shape(fragments, columns)] + back,
            out_specs=[VMEM] * 5,
            scratch_shapes=[pltpu.SemaphoreType.DMA((1,))],
            compiler_params=params(),
            cost_estimate=cost(2 * matmul, 2 * block),
            name="second",
        )(counts, near_core(raw_next), near_core(c_next), far(integrals))
        borders.append(exchange(made_next))
        gain, weights = pl.pallas_call(
            gain_kernel,
            in_specs=[SMEM] * 2 + [VMEM] * 3,
            out_shape=[
                pltpu.VMEM((fragments, columns, virtuals, virtuals), F32),
                jax.ShapeDtypeStruct((2 * WIN, fragments * columns), F32),
            ],
            out_specs=[VMEM] * 2,
            compiler_params=params(),
            cost_estimate=cost(16 * virtuals**2 * pairs, 4 * block),
            name="gain",
        )(*lax.optimization_barrier((occ_energy, counts, pno_energy, listed, occ_fock, tm_next))[:5])
        return [tm, tm_next], [c, c_next], k, [made[0], made_next[0]], borders, weights, gain

    def exchange(made):
        from_far = lax.ppermute(made[2], "ja", far_pairs)
        return lax.ppermute(made[1], "ja", near_pairs), from_far

    def next_step(offset, n, gain, halves, partner, current, coefs):
        return pl.pallas_call(
            partial(middle_kernel, offset, offset % size),
            in_specs=[VMEM] * 5,
            out_shape=[near_shape(n, columns)] + back_shapes(n),
            out_specs=[VMEM] * 4,
            compiler_params=params(),
            cost_estimate=cost(2 * matmul * n // size, block),
            name="middle",
        )(*map(near_core, (gain, halves, partner, current[offset // size], coefs[offset // size])))

    def half_step(offset, weights, amps, coefs, ints, back_form, border, out):
        operands = [amps, coefs[offset // size], ints, back_form, *border]
        aliases = {}
        if out is not None:
            aliases = {len(operands) + 1: 0}
            operands.append(out)
        return pl.pallas_call(
            partial(half_kernel, offset, offset % size),
            in_specs=[SMEM] + [VMEM] * len(operands),
            out_shape=near_shape(columns, fragments),
            out_specs=VMEM,
            scratch_shapes=[pltpu.VMEM((columns + 2 * WIN, virtuals, virtuals), F32)],
            input_output_aliases=aliases,
            compiler_params=params(),
            cost_estimate=cost(4 * matmul * amps.shape[0] // size, 2 * block),
            name="half",
        )(weights, *map(near_core, operands))

    def last_step(gain, halves, partner, current):
        return pl.pallas_call(
            last_kernel,
            in_specs=[VMEM] * (3 + len(current)),
            out_shape=pltpu.HBM(amplitudes.shape, BF),
            out_specs=HBM,
            scratch_shapes=[
                pltpu.VMEM((fragments, columns, virtuals, virtuals), BF),
                pltpu.SemaphoreType.DMA((fragments,)),
            ],
            compiler_params=params(),
            cost_estimate=cost(0, 4 * block),
            name="last",
        )(
            near_core(gain), near_core(halves), near_core(partner),
            *map(near_core, current),
        )

    halves = partner = None
    for sweep in range(ITERS):
        offsets = [sum(GROUPS[sweep][:g]) for g in range(len(GROUPS[sweep]))]
        if sweep == 0:
            current, coefs, ints, back_form, borders, weights, gain = first_steps()
        else:
            new, back_form, borders = [], [], []
            for offset, n in zip(offsets, GROUPS[sweep], strict=True):
                tm, *made = next_step(offset, n, gain, halves, partner, current, coefs)
                borders.append(exchange(made))
                new.append(tm)
                back_form.append(made[0])
            current = new
        halves = None
        for g, offset in enumerate(offsets):
            halves = half_step(
                offset, weights, current[g], coefs, ints, back_form[g], borders[g], halves
            )
        sent = halves.reshape(columns * fragments, 1, virtuals, virtuals)
        arrived = lax.all_to_all(sent, ("ia", "ja"), split_axis=0, concat_axis=0, tiled=True)
        partner = arrived.reshape(columns, fragments, virtuals, virtuals)
    return last_step(gain, halves, partner, current)


def solution(mesh):
    placed = (
        P(None, "ia", "ja", None, None),
        P(None, "ia", "ja", None, None),
        P(None, "ia", "ja", None, None),
        P(None, "ia", "ja", None),
        P(None, "ia", "ja"),
        P(None, "ia", "ja", None),
        P(),
        P(),
    )
    return jax.shard_map(
        on_device,
        mesh=mesh,
        in_specs=placed,
        out_specs=P(None, "ia", "ja", None, None),
        check_vma=False,
    )
```

```python
from functools import partial

import jax
import jax.numpy as jnp
from jax import lax
from jax.experimental import pallas as pl
from jax.experimental.pallas import tpu as pltpu
from jax.sharding import PartitionSpec as P

WIN = 6
ITERS = 2
DAMPING = 0.5
GROUPS = ((4, 4), (4, 2, 2))
SKEW = 4
VMEM_BYTES = 16 * 1024 * 1024

BF = jnp.bfloat16
F32 = jnp.float32


def window_shift(slot_index):
    return slot_index - WIN if slot_index < WIN else slot_index - WIN + 1


def nn(a, b):
    return lax.dot_general(a, b, (((1,), (0,)), ((), ())), preferred_element_type=F32)


def nt(a, b):
    return lax.dot_general(a, b, (((1,), (1,)), ((), ())), preferred_element_type=F32)


def tn(a, b):
    return lax.dot_general(a, b, (((0,), (0,)), ((), ())), preferred_element_type=F32)


def inside_mask(count, virtuals):
    rows = lax.broadcasted_iota(jnp.int32, (virtuals, virtuals), 0)
    cols = lax.broadcasted_iota(jnp.int32, (virtuals, virtuals), 1)
    return jnp.maximum(rows, cols) < count


def back_forms(f, parity, amps, coef, x_ref, near_ref, far_ref):
    columns = x_ref.shape[1]
    ready, leading = {}, {}
    for step in range(columns + 2 * SKEW):
        b = step
        if b < columns:
            ready[b] = amps(b)
        b = step - SKEW
        if 0 <= b < columns:
            leading[b] = nn(coef(b), ready.pop(b)).astype(BF)
        b = step - 2 * SKEW
        if 0 <= b:
            x_ref[f, b] = nt(leading.pop(b), coef(b)).astype(BF)
    edge = columns - WIN
    near_ref[f] = x_ref[f, pl.ds((1 - parity) * edge, WIN)]
    far_ref[f] = x_ref[f, pl.ds(parity * edge, WIN)]


def masked_forms(f, offset, parity, counts_ref, raw_ref, c_ref, tm_ref, x_ref, near_ref, far_ref):
    virtuals = x_ref.shape[2]

    def amps(b):
        keep = inside_mask(counts_ref[f + offset, 0, b], virtuals)
        value = jnp.where(keep, raw_ref[f, b].astype(F32), 0.0).astype(BF)
        tm_ref[f, b] = value
        return value

    back_forms(f, parity, amps, lambda b: c_ref[f, b], x_ref, near_ref, far_ref)


def start_kernel(
    counts_hbm, t_hbm, c_hbm, tm_ref, c_ref, raw_next, c_next, x_ref, near_ref, far_ref,
    raw_ref, counts_ref, sems, next_sems,
):
    size = x_ref.shape[0]
    parity = lax.rem(lax.axis_index("ja"), 2)

    def loads(f):
        return (
            pltpu.make_async_copy(t_hbm.at[f, 0], raw_ref.at[f], sems.at[f, 0]),
            pltpu.make_async_copy(c_hbm.at[f, 0], c_ref.at[f], sems.at[f, 1]),
        )

    for f in range(size):
        for load in loads(f):
            load.start()
    number = pltpu.make_async_copy(counts_hbm, counts_ref, next_sems.at[2])
    number.start()
    rest = pl.ds(size, size)
    later = (
        pltpu.make_async_copy(t_hbm.at[rest, 0], raw_next, next_sems.at[0]),
        pltpu.make_async_copy(c_hbm.at[rest, 0], c_next, next_sems.at[1]),
    )
    for load in later:
        load.start()
    number.wait()

    def body(f, carry):
        for load in loads(f):
            load.wait()
        masked_forms(f, 0, parity, counts_ref, raw_ref, c_ref, tm_ref, x_ref, near_ref, far_ref)
        return carry

    lax.fori_loop(0, size, body, 0)
    for load in later:
        load.wait()


def second_kernel(
    counts_ref, raw_ref, c_ref, k_hbm, tm_ref, k_ref, x_ref, near_ref, far_ref, sems
):
    size = x_ref.shape[0]
    parity = lax.rem(lax.axis_index("ja"), 2)
    load = pltpu.make_async_copy(k_hbm.at[:, 0], k_ref, sems.at[0])
    load.start()

    def body(f, carry):
        masked_forms(f, size, parity, counts_ref, raw_ref, c_ref, tm_ref, x_ref, near_ref, far_ref)
        return carry

    lax.fori_loop(0, size, body, 0)
    load.wait()


def gain_kernel(occ_ref, counts_ref, e_ref, coupled_ref, fock_ref, gain_ref, w_ref):
    orbitals = fock_ref.shape[0]
    fragments, columns, virtuals = gain_ref.shape[:3]
    slots = 2 * WIN
    rows = lax.broadcasted_iota(jnp.int32, (orbitals, orbitals), 0)
    cols = lax.broadcasted_iota(jnp.int32, (orbitals, orbitals), 1)
    turn = lax.rem(orbitals - lax.axis_index("ja") * columns, orbitals)
    for s in range(slots):
        band = jnp.where(rows == cols + window_shift(s), fock_ref[...], 0.0)
        band = pltpu.roll(jnp.sum(band, axis=0, keepdims=True), turn, 1)[:, :columns]
        parts = [coupled_ref[f * slots + s].astype(F32) * band for f in range(fragments)]
        w_ref[s : s + 1, :] = -virtuals * jnp.concatenate(parts, axis=1)

    def body(f, carry):
        rows_energy = e_ref[f, 0].T
        occ_row = occ_ref[f * columns + lax.axis_index("ia")]
        for b in range(columns):
            occ_col = occ_ref[lax.axis_index("ja") * columns + b]
            cols_energy = e_ref[f, 0, b : b + 1, :] - occ_col
            denominator = (rows_energy[:, b : b + 1] - occ_row) + cols_energy
            keep = inside_mask(counts_ref[f, 0, b], virtuals)
            gain_ref[f, b] = jnp.where(keep, (DAMPING / virtuals) * pl.reciprocal(denominator), 0.0)
        return carry

    lax.fori_loop(0, fragments, body, 0)


def updated(f, b, amps, gain_ref, h_ref, p_ref):
    residual = h_ref[b, f].astype(F32) + p_ref[b, f].T.astype(F32)
    return ((1.0 - DAMPING) * amps.astype(F32) - gain_ref[f, b] * residual).astype(BF)


def middle_kernel(
    offset, inner, gain_ref, h_ref, p_ref, t_ref, c_ref,
    tm_ref, x_ref, near_ref, far_ref,
):
    parity = lax.rem(lax.axis_index("ja"), 2)

    def body(f, carry):
        def amps(b):
            value = updated(f + offset, b, t_ref[f + inner, b], gain_ref, h_ref, p_ref)
            tm_ref[f, b] = value
            return value

        back_forms(f, parity, amps, lambda b: c_ref[f + inner, b], x_ref, near_ref, far_ref)
        return carry

    lax.fori_loop(0, x_ref.shape[0], body, 0)


def last_kernel(gain_ref, h_ref, p_ref, *rest):
    out_hbm, made_ref, sems = rest[-3:]
    columns = made_ref.shape[1]

    def store(f):
        return pltpu.make_async_copy(made_ref.at[f], out_hbm.at[f, 0], sems.at[f])

    offset = 0
    for t_ref in rest[:-3]:

        def body(f, carry, offset=offset, t_ref=t_ref):
            for b in range(columns):
                made_ref[f + offset, b] = updated(
                    f + offset, b, t_ref[f, b], gain_ref, h_ref, p_ref
                )
            store(f + offset).start()
            return carry

        lax.fori_loop(0, t_ref.shape[0], body, 0)
        offset += t_ref.shape[0]
    for f in range(offset):
        store(f).wait()


def half_kernel(offset, inner, w_ref, t_ref, c_ref, k_ref, x_ref, near_ref, far_ref, *rest):
    h_ref, xf = rest[-2:]
    size, columns, virtuals = x_ref.shape[:3]
    lag = columns // 2
    parity = lax.rem(lax.axis_index("ja"), 2)

    def body(f, carry):
        xf[pl.ds((1 - parity) * (WIN + columns), WIN)] = near_ref[f].astype(F32)
        xf[pl.ds(parity * (WIN + columns), WIN)] = far_ref[f].astype(F32)
        xf[WIN : WIN + columns] = x_ref[f].astype(F32)
        window, left_proj, left_quad = {}, {}, {}
        for step in range(columns + 2 * lag):
            b = step
            if b < columns:
                total = w_ref[0, (f + offset) * columns + b] * xf[b + WIN + window_shift(0)]
                for s in range(1, 2 * WIN):
                    total = total + w_ref[s, (f + offset) * columns + b] * xf[b + WIN + window_shift(s)]
                window[b] = total.astype(BF)
            b = step - lag
            if 0 <= b < columns:
                left_proj[b] = tn(window.pop(b), c_ref[f + inner, b]).astype(BF)
                left_quad[b] = nn(t_ref[f, b], k_ref[f + offset, b]).astype(BF)
            b = step - 2 * lag
            if 0 <= b:
                joined = tn(left_proj.pop(b), c_ref[f + inner, b]) + nn(left_quad.pop(b), t_ref[f, b])
                scaled = (0.5 * virtuals) * k_ref[f + offset, b].astype(F32)
                h_ref[b, f + offset] = (scaled + joined).astype(BF)
        return carry

    lax.fori_loop(0, size, body, 0)


SMEM = pl.BlockSpec(memory_space=pltpu.SMEM)
VMEM = pl.BlockSpec(memory_space=pltpu.VMEM)
HBM = pl.BlockSpec(memory_space=pltpu.HBM)


def params():
    return pltpu.CompilerParams(vmem_limit_bytes=VMEM_BYTES)


def near_core(value):
    return pltpu.with_memory_space_constraint(value, pltpu.VMEM)


def far(value):
    return pltpu.with_memory_space_constraint(value, pltpu.HBM)


def cost(flops, moved):
    return pl.CostEstimate(flops=flops, bytes_accessed=moved, transcendentals=0)


def on_device(
    amplitudes, coefficients, integrals, pno_energy, pno_counts, coupled, occ_fock, occ_energy
):
    fragments, _, columns, virtuals, _ = amplitudes.shape
    size = fragments // 2
    pairs = size * columns
    matmul = 2 * virtuals**3 * pairs
    block = 2 * virtuals**2 * pairs
    listed = jnp.transpose(coupled, (0, 3, 1, 2)).reshape(fragments * 2 * WIN, 1, columns)
    counts = pno_counts

    peers = lax.axis_size("ja")
    near_pairs = [(i, i ^ 1) for i in range(peers)]
    far_pairs = [(i, i + 1 if i % 2 else i - 1) for i in range(1, peers - 1)]

    def near_shape(*lead):
        return pltpu.VMEM((*lead, virtuals, virtuals), BF)

    def back_shapes(n):
        return [near_shape(n, m) for m in (columns, WIN, WIN)]

    group, back = near_shape(size, columns), back_shapes(size)

    def first_steps():
        tm, c, raw_next, c_next, *made = pl.pallas_call(
            start_kernel,
            in_specs=[HBM, HBM, HBM],
            out_shape=[group] * 4 + back,
            out_specs=[VMEM] * 7,
            scratch_shapes=[
                pltpu.VMEM((size, columns, virtuals, virtuals), BF),
                pltpu.SMEM(counts.shape, jnp.int32),
                pltpu.SemaphoreType.DMA((size, 2)),
                pltpu.SemaphoreType.DMA((3,)),
            ],
            compiler_params=params(),
            cost_estimate=cost(2 * matmul, 4 * block),
            name="start",
        )(far(counts), far(amplitudes), far(coefficients))
        borders = [exchange(made)]
        tm_next, k, *made_next = pl.pallas_call(
            second_kernel,
            in_specs=[SMEM, VMEM, VMEM, HBM],
            out_shape=[group, near_shape(fragments, columns)] + back,
            out_specs=[VMEM] * 5,
            scratch_shapes=[pltpu.SemaphoreType.DMA((1,))],
            compiler_params=params(),
            cost_estimate=cost(2 * matmul, 2 * block),
            name="second",
        )(counts, near_core(raw_next), near_core(c_next), far(integrals))
        borders.append(exchange(made_next))
        gain, weights = pl.pallas_call(
            gain_kernel,
            in_specs=[SMEM] * 2 + [VMEM] * 3,
            out_shape=[
                pltpu.VMEM((fragments, columns, virtuals, virtuals), F32),
                jax.ShapeDtypeStruct((2 * WIN, fragments * columns), F32),
            ],
            out_specs=[VMEM] * 2,
            compiler_params=params(),
            cost_estimate=cost(16 * virtuals**2 * pairs, 4 * block),
            name="gain",
        )(*lax.optimization_barrier((occ_energy, counts, pno_energy, listed, occ_fock, tm_next))[:5])
        return [tm, tm_next], [c, c_next], k, [made[0], made_next[0]], borders, weights, gain

    def exchange(made):
        from_far = lax.ppermute(made[2], "ja", far_pairs)
        return lax.ppermute(made[1], "ja", near_pairs), from_far

    def next_step(offset, n, gain, halves, partner, current, coefs):
        return pl.pallas_call(
            partial(middle_kernel, offset, offset % size),
            in_specs=[VMEM] * 5,
            out_shape=[near_shape(n, columns)] + back_shapes(n),
            out_specs=[VMEM] * 4,
            compiler_params=params(),
            cost_estimate=cost(2 * matmul * n // size, block),
            name="middle",
        )(*map(near_core, (gain, halves, partner, current[offset // size], coefs[offset // size])))

    def half_step(offset, weights, amps, coefs, ints, back_form, border, out):
        operands = [amps, coefs[offset // size], ints, back_form, *border]
        aliases = {}
        if out is not None:
            aliases = {len(operands) + 1: 0}
            operands.append(out)
        return pl.pallas_call(
            partial(half_kernel, offset, offset % size),
            in_specs=[SMEM] + [VMEM] * len(operands),
            out_shape=near_shape(columns, fragments),
            out_specs=VMEM,
            scratch_shapes=[pltpu.VMEM((columns + 2 * WIN, virtuals, virtuals), F32)],
            input_output_aliases=aliases,
            compiler_params=params(),
            cost_estimate=cost(4 * matmul * amps.shape[0] // size, 2 * block),
            name="half",
        )(weights, *map(near_core, operands))

    def last_step(gain, halves, partner, current):
        return pl.pallas_call(
            last_kernel,
            in_specs=[VMEM] * (3 + len(current)),
            out_shape=pltpu.HBM(amplitudes.shape, BF),
            out_specs=HBM,
            scratch_shapes=[
                pltpu.VMEM((fragments, columns, virtuals, virtuals), BF),
                pltpu.SemaphoreType.DMA((fragments,)),
            ],
            compiler_params=params(),
            cost_estimate=cost(0, 4 * block),
            name="last",
        )(
            near_core(gain), near_core(halves), near_core(partner),
            *map(near_core, current),
        )

    halves = partner = None
    for sweep in range(ITERS):
        offsets = [sum(GROUPS[sweep][:g]) for g in range(len(GROUPS[sweep]))]
        if sweep == 0:
            current, coefs, ints, back_form, borders, weights, gain = first_steps()
        else:
            new, back_form, borders = [], [], []
            for offset, n in zip(offsets, GROUPS[sweep], strict=True):
                tm, *made = next_step(offset, n, gain, halves, partner, current, coefs)
                borders.append(exchange(made))
                new.append(tm)
                back_form.append(made[0])
            current = new
        halves = None
        for g, offset in enumerate(offsets):
            halves = half_step(
                offset, weights, current[g], coefs, ints, back_form[g], borders[g], halves
            )
        sent = halves.reshape(columns * fragments, 1, virtuals, virtuals)
        arrived = lax.all_to_all(sent, ("ia", "ja"), split_axis=0, concat_axis=0, tiled=True)
        partner = arrived.reshape(columns, fragments, virtuals, virtuals)
    return last_step(gain, halves, partner, current)


def solution(mesh):
    placed = (
        P(None, "ia", "ja", None, None),
        P(None, "ia", "ja", None, None),
        P(None, "ia", "ja", None, None),
        P(None, "ia", "ja", None),
        P(None, "ia", "ja"),
        P(None, "ia", "ja", None),
        P(),
        P(),
    )
    return jax.shard_map(
        on_device,
        mesh=mesh,
        in_specs=placed,
        out_specs=P(None, "ia", "ja", None, None),
        check_vma=False,
    )
```

```python
from functools import partial

import jax
import jax.numpy as jnp
from jax import lax
from jax.experimental import pallas as pl
from jax.experimental.pallas import tpu as pltpu
from jax.sharding import PartitionSpec as P

WIN = 6
ITERS = 2
DAMPING = 0.5
GROUPS = ((4, 4), (4, 2, 2))
SKEW = 6
VMEM_BYTES = 16 * 1024 * 1024

BF = jnp.bfloat16
F32 = jnp.float32


def window_shift(slot_index):
    return slot_index - WIN if slot_index < WIN else slot_index - WIN + 1


def nn(a, b):
    return lax.dot_general(a, b, (((1,), (0,)), ((), ())), preferred_element_type=F32)


def nt(a, b):
    return lax.dot_general(a, b, (((1,), (1,)), ((), ())), preferred_element_type=F32)


def tn(a, b):
    return lax.dot_general(a, b, (((0,), (0,)), ((), ())), preferred_element_type=F32)


def inside_mask(count, virtuals):
    rows = lax.broadcasted_iota(jnp.int32, (virtuals, virtuals), 0)
    cols = lax.broadcasted_iota(jnp.int32, (virtuals, virtuals), 1)
    return jnp.maximum(rows, cols) < count


def back_forms(f, parity, amps, coef, x_ref, near_ref, far_ref):
    columns = x_ref.shape[1]
    ready, leading = {}, {}
    for step in range(columns + 2 * SKEW):
        b = step
        if b < columns:
            ready[b] = amps(b)
        b = step - SKEW
        if 0 <= b < columns:
            leading[b] = nn(coef(b), ready.pop(b)).astype(BF)
        b = step - 2 * SKEW
        if 0 <= b:
            x_ref[f, b] = nt(leading.pop(b), coef(b)).astype(BF)
    edge = columns - WIN
    near_ref[f] = x_ref[f, pl.ds((1 - parity) * edge, WIN)]
    far_ref[f] = x_ref[f, pl.ds(parity * edge, WIN)]


def masked_forms(f, offset, parity, counts_ref, raw_ref, c_ref, tm_ref, x_ref, near_ref, far_ref):
    virtuals = x_ref.shape[2]

    def amps(b):
        keep = inside_mask(counts_ref[f + offset, 0, b], virtuals)
        value = jnp.where(keep, raw_ref[f, b].astype(F32), 0.0).astype(BF)
        tm_ref[f, b] = value
        return value

    back_forms(f, parity, amps, lambda b: c_ref[f, b], x_ref, near_ref, far_ref)


def start_kernel(
    counts_hbm, t_hbm, c_hbm, tm_ref, c_ref, raw_next, c_next, x_ref, near_ref, far_ref,
    raw_ref, counts_ref, sems, next_sems,
):
    size = x_ref.shape[0]
    parity = lax.rem(lax.axis_index("ja"), 2)

    def loads(f):
        return (
            pltpu.make_async_copy(t_hbm.at[f, 0], raw_ref.at[f], sems.at[f, 0]),
            pltpu.make_async_copy(c_hbm.at[f, 0], c_ref.at[f], sems.at[f, 1]),
        )

    for f in range(size):
        for load in loads(f):
            load.start()
    number = pltpu.make_async_copy(counts_hbm, counts_ref, next_sems.at[2])
    number.start()
    rest = pl.ds(size, size)
    later = (
        pltpu.make_async_copy(t_hbm.at[rest, 0], raw_next, next_sems.at[0]),
        pltpu.make_async_copy(c_hbm.at[rest, 0], c_next, next_sems.at[1]),
    )
    for load in later:
        load.start()
    number.wait()

    def body(f, carry):
        for load in loads(f):
            load.wait()
        masked_forms(f, 0, parity, counts_ref, raw_ref, c_ref, tm_ref, x_ref, near_ref, far_ref)
        return carry

    lax.fori_loop(0, size, body, 0)
    for load in later:
        load.wait()


def second_kernel(
    counts_ref, raw_ref, c_ref, k_hbm, tm_ref, k_ref, x_ref, near_ref, far_ref, sems
):
    size = x_ref.shape[0]
    parity = lax.rem(lax.axis_index("ja"), 2)
    load = pltpu.make_async_copy(k_hbm.at[:, 0], k_ref, sems.at[0])
    load.start()

    def body(f, carry):
        masked_forms(f, size, parity, counts_ref, raw_ref, c_ref, tm_ref, x_ref, near_ref, far_ref)
        return carry

    lax.fori_loop(0, size, body, 0)
    load.wait()


def gain_kernel(occ_ref, counts_ref, e_ref, coupled_ref, fock_ref, gain_ref, w_ref):
    orbitals = fock_ref.shape[0]
    fragments, columns, virtuals = gain_ref.shape[:3]
    slots = 2 * WIN
    rows = lax.broadcasted_iota(jnp.int32, (orbitals, orbitals), 0)
    cols = lax.broadcasted_iota(jnp.int32, (orbitals, orbitals), 1)
    turn = lax.rem(orbitals - lax.axis_index("ja") * columns, orbitals)
    for s in range(slots):
        band = jnp.where(rows == cols + window_shift(s), fock_ref[...], 0.0)
        band = pltpu.roll(jnp.sum(band, axis=0, keepdims=True), turn, 1)[:, :columns]
        parts = [coupled_ref[f * slots + s].astype(F32) * band for f in range(fragments)]
        w_ref[s : s + 1, :] = -virtuals * jnp.concatenate(parts, axis=1)

    def body(f, carry):
        rows_energy = e_ref[f, 0].T
        occ_row = occ_ref[f * columns + lax.axis_index("ia")]
        for b in range(columns):
            occ_col = occ_ref[lax.axis_index("ja") * columns + b]
            cols_energy = e_ref[f, 0, b : b + 1, :] - occ_col
            denominator = (rows_energy[:, b : b + 1] - occ_row) + cols_energy
            keep = inside_mask(counts_ref[f, 0, b], virtuals)
            gain_ref[f, b] = jnp.where(keep, (DAMPING / virtuals) * pl.reciprocal(denominator), 0.0)
        return carry

    lax.fori_loop(0, fragments, body, 0)


def updated(f, b, amps, gain_ref, h_ref, p_ref):
    residual = h_ref[b, f].astype(F32) + p_ref[b, f].T.astype(F32)
    return ((1.0 - DAMPING) * amps.astype(F32) - gain_ref[f, b] * residual).astype(BF)


def middle_kernel(
    offset, inner, gain_ref, h_ref, p_ref, t_ref, c_ref,
    tm_ref, x_ref, near_ref, far_ref,
):
    parity = lax.rem(lax.axis_index("ja"), 2)

    def body(f, carry):
        def amps(b):
            value = updated(f + offset, b, t_ref[f + inner, b], gain_ref, h_ref, p_ref)
            tm_ref[f, b] = value
            return value

        back_forms(f, parity, amps, lambda b: c_ref[f + inner, b], x_ref, near_ref, far_ref)
        return carry

    lax.fori_loop(0, x_ref.shape[0], body, 0)


def last_kernel(gain_ref, h_ref, p_ref, *rest):
    out_hbm, made_ref, sems = rest[-3:]
    columns = made_ref.shape[1]

    def store(f):
        return pltpu.make_async_copy(made_ref.at[f], out_hbm.at[f, 0], sems.at[f])

    offset = 0
    for t_ref in rest[:-3]:

        def body(f, carry, offset=offset, t_ref=t_ref):
            for b in range(columns):
                made_ref[f + offset, b] = updated(
                    f + offset, b, t_ref[f, b], gain_ref, h_ref, p_ref
                )
            store(f + offset).start()
            return carry

        lax.fori_loop(0, t_ref.shape[0], body, 0)
        offset += t_ref.shape[0]
    for f in range(offset):
        store(f).wait()


def half_kernel(offset, inner, w_ref, t_ref, c_ref, k_ref, x_ref, near_ref, far_ref, *rest):
    h_ref, xf = rest[-2:]
    size, columns, virtuals = x_ref.shape[:3]
    lag = columns // 2
    parity = lax.rem(lax.axis_index("ja"), 2)

    def body(f, carry):
        xf[pl.ds((1 - parity) * (WIN + columns), WIN)] = near_ref[f].astype(F32)
        xf[pl.ds(parity * (WIN + columns), WIN)] = far_ref[f].astype(F32)
        xf[WIN : WIN + columns] = x_ref[f].astype(F32)
        window, left_proj, left_quad = {}, {}, {}
        for step in range(columns + 2 * lag):
            b = step
            if b < columns:
                total = w_ref[0, (f + offset) * columns + b] * xf[b + WIN + window_shift(0)]
                for s in range(1, 2 * WIN):
                    total = total + w_ref[s, (f + offset) * columns + b] * xf[b + WIN + window_shift(s)]
                window[b] = total.astype(BF)
            b = step - lag
            if 0 <= b < columns:
                left_proj[b] = tn(window.pop(b), c_ref[f + inner, b]).astype(BF)
                left_quad[b] = nn(t_ref[f, b], k_ref[f + offset, b]).astype(BF)
            b = step - 2 * lag
            if 0 <= b:
                joined = tn(left_proj.pop(b), c_ref[f + inner, b]) + nn(left_quad.pop(b), t_ref[f, b])
                scaled = (0.5 * virtuals) * k_ref[f + offset, b].astype(F32)
                h_ref[b, f + offset] = (scaled + joined).astype(BF)
        return carry

    lax.fori_loop(0, size, body, 0)


SMEM = pl.BlockSpec(memory_space=pltpu.SMEM)
VMEM = pl.BlockSpec(memory_space=pltpu.VMEM)
HBM = pl.BlockSpec(memory_space=pltpu.HBM)


def params():
    return pltpu.CompilerParams(vmem_limit_bytes=VMEM_BYTES)


def near_core(value):
    return pltpu.with_memory_space_constraint(value, pltpu.VMEM)


def far(value):
    return pltpu.with_memory_space_constraint(value, pltpu.HBM)


def cost(flops, moved):
    return pl.CostEstimate(flops=flops, bytes_accessed=moved, transcendentals=0)


def on_device(
    amplitudes, coefficients, integrals, pno_energy, pno_counts, coupled, occ_fock, occ_energy
):
    fragments, _, columns, virtuals, _ = amplitudes.shape
    size = fragments // 2
    pairs = size * columns
    matmul = 2 * virtuals**3 * pairs
    block = 2 * virtuals**2 * pairs
    listed = jnp.transpose(coupled, (0, 3, 1, 2)).reshape(fragments * 2 * WIN, 1, columns)
    counts = pno_counts

    peers = lax.axis_size("ja")
    near_pairs = [(i, i ^ 1) for i in range(peers)]
    far_pairs = [(i, i + 1 if i % 2 else i - 1) for i in range(1, peers - 1)]

    def near_shape(*lead):
        return pltpu.VMEM((*lead, virtuals, virtuals), BF)

    def back_shapes(n):
        return [near_shape(n, m) for m in (columns, WIN, WIN)]

    group, back = near_shape(size, columns), back_shapes(size)

    def first_steps():
        tm, c, raw_next, c_next, *made = pl.pallas_call(
            start_kernel,
            in_specs=[HBM, HBM, HBM],
            out_shape=[group] * 4 + back,
            out_specs=[VMEM] * 7,
            scratch_shapes=[
                pltpu.VMEM((size, columns, virtuals, virtuals), BF),
                pltpu.SMEM(counts.shape, jnp.int32),
                pltpu.SemaphoreType.DMA((size, 2)),
                pltpu.SemaphoreType.DMA((3,)),
            ],
            compiler_params=params(),
            cost_estimate=cost(2 * matmul, 4 * block),
            name="start",
        )(far(counts), far(amplitudes), far(coefficients))
        borders = [exchange(made)]
        tm_next, k, *made_next = pl.pallas_call(
            second_kernel,
            in_specs=[SMEM, VMEM, VMEM, HBM],
            out_shape=[group, near_shape(fragments, columns)] + back,
            out_specs=[VMEM] * 5,
            scratch_shapes=[pltpu.SemaphoreType.DMA((1,))],
            compiler_params=params(),
            cost_estimate=cost(2 * matmul, 2 * block),
            name="second",
        )(counts, near_core(raw_next), near_core(c_next), far(integrals))
        borders.append(exchange(made_next))
        gain, weights = pl.pallas_call(
            gain_kernel,
            in_specs=[SMEM] * 2 + [VMEM] * 3,
            out_shape=[
                pltpu.VMEM((fragments, columns, virtuals, virtuals), F32),
                jax.ShapeDtypeStruct((2 * WIN, fragments * columns), F32),
            ],
            out_specs=[VMEM] * 2,
            compiler_params=params(),
            cost_estimate=cost(16 * virtuals**2 * pairs, 4 * block),
            name="gain",
        )(*lax.optimization_barrier((occ_energy, counts, pno_energy, listed, occ_fock, tm_next))[:5])
        return [tm, tm_next], [c, c_next], k, [made[0], made_next[0]], borders, weights, gain

    def exchange(made):
        from_far = lax.ppermute(made[2], "ja", far_pairs)
        return lax.ppermute(made[1], "ja", near_pairs), from_far

    def next_step(offset, n, gain, halves, partner, current, coefs):
        return pl.pallas_call(
            partial(middle_kernel, offset, offset % size),
            in_specs=[VMEM] * 5,
            out_shape=[near_shape(n, columns)] + back_shapes(n),
            out_specs=[VMEM] * 4,
            compiler_params=params(),
            cost_estimate=cost(2 * matmul * n // size, block),
            name="middle",
        )(*map(near_core, (gain, halves, partner, current[offset // size], coefs[offset // size])))

    def half_step(offset, weights, amps, coefs, ints, back_form, border, out):
        operands = [amps, coefs[offset // size], ints, back_form, *border]
        aliases = {}
        if out is not None:
            aliases = {len(operands) + 1: 0}
            operands.append(out)
        return pl.pallas_call(
            partial(half_kernel, offset, offset % size),
            in_specs=[SMEM] + [VMEM] * len(operands),
            out_shape=near_shape(columns, fragments),
            out_specs=VMEM,
            scratch_shapes=[pltpu.VMEM((columns + 2 * WIN, virtuals, virtuals), F32)],
            input_output_aliases=aliases,
            compiler_params=params(),
            cost_estimate=cost(4 * matmul * amps.shape[0] // size, 2 * block),
            name="half",
        )(weights, *map(near_core, operands))

    def last_step(gain, halves, partner, current):
        return pl.pallas_call(
            last_kernel,
            in_specs=[VMEM] * (3 + len(current)),
            out_shape=pltpu.HBM(amplitudes.shape, BF),
            out_specs=HBM,
            scratch_shapes=[
                pltpu.VMEM((fragments, columns, virtuals, virtuals), BF),
                pltpu.SemaphoreType.DMA((fragments,)),
            ],
            compiler_params=params(),
            cost_estimate=cost(0, 4 * block),
            name="last",
        )(
            near_core(gain), near_core(halves), near_core(partner),
            *map(near_core, current),
        )

    halves = partner = None
    for sweep in range(ITERS):
        offsets = [sum(GROUPS[sweep][:g]) for g in range(len(GROUPS[sweep]))]
        if sweep == 0:
            current, coefs, ints, back_form, borders, weights, gain = first_steps()
        else:
            new, back_form, borders = [], [], []
            for offset, n in zip(offsets, GROUPS[sweep], strict=True):
                tm, *made = next_step(offset, n, gain, halves, partner, current, coefs)
                borders.append(exchange(made))
                new.append(tm)
                back_form.append(made[0])
            current = new
        halves = None
        for g, offset in enumerate(offsets):
            halves = half_step(
                offset, weights, current[g], coefs, ints, back_form[g], borders[g], halves
            )
        sent = halves.reshape(columns * fragments, 1, virtuals, virtuals)
        arrived = lax.all_to_all(sent, ("ia", "ja"), split_axis=0, concat_axis=0, tiled=True)
        partner = arrived.reshape(columns, fragments, virtuals, virtuals)
    return last_step(gain, halves, partner, current)


def solution(mesh):
    placed = (
        P(None, "ia", "ja", None, None),
        P(None, "ia", "ja", None, None),
        P(None, "ia", "ja", None, None),
        P(None, "ia", "ja", None),
        P(None, "ia", "ja"),
        P(None, "ia", "ja", None),
        P(),
        P(),
    )
    return jax.shard_map(
        on_device,
        mesh=mesh,
        in_specs=placed,
        out_specs=P(None, "ia", "ja", None, None),
        check_vma=False,
    )
```
